32 devices in a mesh: section: 2 (over x), fsdp: 4 (over y, core), ctx: 4 (over z).
Axes of the slice: x: 2, y: 2, z: 4, core: 2. Of those that a mesh axis runs over, the one named last changes fastest.
Arguments:
- tokens: bfloat16 [2, 4096, 576], P(None, ('fsdp', 'ctx')), may hold values from -6 to 6
- cotangent: bfloat16 [2, 4096, 576], P(None, ('fsdp', 'ctx')), may hold values from -6 to 6
- doc_lengths: int32 [2, 4, 3], P(None, 'fsdp'), may hold values from 1 to 1022, as said below
- norm_gains: bfloat16 [2, 2, 576], P('section', None, ('fsdp', 'ctx')), may hold values from 0.5 to 1.5
- w_qkv: bfloat16 [2, 576, 960], P('section', ('fsdp', 'ctx')), may hold values from -0.25 to 0.25
- w_out: bfloat16 [2, 576, 576], P('section', ('fsdp', 'ctx')), may hold values from -4 to 4
- w_gate_up: bfloat16 [2, 576, 3072], P('section', ('fsdp', 'ctx')), may hold values from -0.25 to 0.25
- w_down: bfloat16 [2, 1536, 576], P('section', ('fsdp', 'ctx')), may hold values from -0.15625 to 0.15625
Outputs:
- activations: bfloat16 [2, 2, 4096, 576], P('section', None, ('fsdp', 'ctx'))
- input_grads: float32 [2, 2, 4096, 576], P('section', None, ('fsdp', 'ctx'))
- grad_attn_gains: float32 [2, 576], P('section', ('fsdp', 'ctx'))
- grad_ffn_gains: float32 [2, 576], P('section', ('fsdp', 'ctx'))
- grad_w_qkv: float32 [2, 576, 960], P('section', ('fsdp', 'ctx'))
- grad_w_out: float32 [2, 576, 576], P('section', ('fsdp', 'ctx'))
- grad_w_gate_up: float32 [2, 576, 3072], P('section', ('fsdp', 'ctx'))
- grad_w_down: float32 [2, 1536, 576], P('section', ('fsdp', 'ctx'))
The draws below stay inside these ranges and needn't reach their ends.
Inputs may be any that keep to these rules, and one draw needn't show every extreme that they name: `doc_lengths`: each packed row holds three sequences whose lengths sum to 1024; the second one starts on the first index of ctx and ends on the last.
All inputs are finite; a program needn't handle non-finite values.
Results may differ from the reference program's by a relative error of at most 0.015.
Values may be sent and summed in bfloat16 or wider, within the bound.
A program may use at most 128 MiB of HBM per device.

```python
import jax
import jax.numpy as jnp
from jax import lax

D = 576
HEADS = 9
KV = 3
HD = 64
FF = 1536
PACK = 1024
MB = 2
TOK_DEV = 256
ROWS = 4096
QKV_W = 960


def draw_doc_lengths(key, part):
    key = jax.random.fold_in(key, 17)
    head_key, tail_key, pick_key = jax.random.split(key, 3)
    row_total = MB * (ROWS // PACK)
    head_lens = jax.random.randint(head_key, (row_total,), 1, TOK_DEV // 2 + 1)
    tail_lens = jax.random.randint(tail_key, (row_total,), 1, TOK_DEV // 2 + 1)
    chosen = jax.random.randint(pick_key, (), 0, row_total)
    places = jnp.arange(row_total)
    head_lens = jnp.where(places == chosen, 1, head_lens)
    tail_lens = jnp.where(places == chosen, 1, tail_lens)
    middle = PACK - head_lens - tail_lens
    return jnp.stack([head_lens, middle, tail_lens], -1).reshape(MB, ROWS // PACK, 3).astype(jnp.int32)


def shard_levels(rng, extent, cuts, low, high):
    loudness, own = 1.0, jax.random.fold_in(rng, 6)
    for dim, blocks in cuts:
        heights = jnp.exp(jax.random.uniform(jax.random.fold_in(own, dim), (blocks,), jnp.float32, low / len(cuts), high / len(cuts)))
        loudness = loudness * jnp.repeat(heights, extent[dim] // blocks).reshape([-1 if axis == dim else 1 for axis in range(len(extent))])
    return loudness


def noise(key, extent, spread, bound, shards=(), kind=jnp.bfloat16):
    drawn = spread * jax.random.normal(key, extent, jnp.float32)
    if shards:
        drawn = drawn * shard_levels(key, extent, shards, -0.22, 0.18)
    return jnp.clip(drawn, -bound, bound).astype(kind)


def setup_inputs(seed: int = 0) -> dict:
    splits = jax.random.split(jax.random.key(seed), 9)
    tokens = noise(splits[0], (MB, ROWS, D), 1.0, 6.0, ((1, 16),))
    cotangent = noise(splits[1], (MB, ROWS, D), 1.0, 6.0, ((1, 16),))
    doc_lengths = draw_doc_lengths(jax.random.fold_in(splits[8], 71), 0)
    norm_gains = jnp.clip(1.0 + 0.1 * jax.random.normal(splits[3], (2, 2, D), jnp.float32), 0.5, 1.5).astype(jnp.bfloat16)
    w_qkv = noise(splits[4], (2, D, QKV_W), D ** -0.5, 0.25, ((0, 2), (1, 16)))
    w_out = noise(splits[5], (2, HEADS * HD, D), 0.7, 4.0, ((0, 2), (1, 16)))
    w_gate_up = noise(splits[6], (2, D, 2 * FF), D ** -0.5, 0.25, ((0, 2), (1, 16)))
    w_down = noise(splits[7], (2, FF, D), FF ** -0.5, 0.15625, ((0, 2), (1, 16)))
    return dict(tokens=tokens, cotangent=cotangent, doc_lengths=doc_lengths, norm_gains=norm_gains, w_qkv=w_qkv, w_out=w_out, w_gate_up=w_gate_up, w_down=w_down)


EPSILON = 1e-05
ROPE_BASE = 100000.0
MASKED = -1e+30
PRECISE = lax.Precision.HIGHEST

@jax.custom_vjp
def low(v):
    return lax.optimization_barrier(v.astype(jnp.bfloat16)).astype(jnp.float32)

@jax.custom_vjp
def low_back(v):
    return v

def low_keep(v):
    return (low(v), None)

def low_pass(kept, grad):
    return (grad,)

def back_keep(v):
    return (v, None)

def back_low(kept, grad):
    return (low(grad),)
low.defvjp(low_keep, low_pass)
low_back.defvjp(back_keep, back_low)

def matmul(left_side, right_side):
    return jnp.dot(left_side, right_side, preferred_element_type=jnp.float32, precision=PRECISE)

def norm_scale(values, norm_gain):
    return values * lax.rsqrt(lax.optimization_barrier(jnp.mean(values * values, -1, keepdims=True)) + EPSILON) * norm_gain

def rotate(values, docpos):
    half_size = values.shape[-1] // 2
    frequency = ROPE_BASE ** (-(jnp.arange(half_size, dtype=jnp.float32) * 2.0 / values.shape[-1]))
    angles = docpos[:, None] * frequency[None, :]
    cosine = jnp.cos(angles)[:, None, :]
    sine_rows = jnp.sin(angles)[:, None, :]
    lower_half = values[..., :half_size]
    upper_half = values[..., half_size:]
    return jnp.concatenate([lower_half * cosine - upper_half * sine_rows, upper_half * cosine + lower_half * sine_rows], -1)

def layout(lengths, pack_len):
    seq_ends = jnp.cumsum(lengths).astype(jnp.int32)
    starts = (seq_ends - lengths).astype(jnp.int32)
    places = jnp.arange(pack_len, dtype=jnp.int32)
    segment = lax.optimization_barrier(jnp.sum((places[:, None] >= seq_ends[None, :2]).astype(jnp.int32), -1)).astype(jnp.int32)
    owners = segment[:, None] == jnp.arange(3, dtype=jnp.int32)[None, :]
    begins = lax.optimization_barrier(jnp.sum(jnp.where(owners, starts[None, :], 0), -1)).astype(jnp.int32)
    docpos = (places - begins).astype(jnp.float32)
    return (segment, docpos)

def attention(queries, key_rows, value_rows, segment):
    length = queries.shape[0]
    block_len = min(length, 512)
    block_count = length // block_len
    groups = HEADS // KV
    score_scale = HD ** (-0.5)
    places = jnp.arange(length, dtype=jnp.int32)

    def one_block(operands):
        query_block, seg_block, place_block = operands
        scores = low_back(jnp.einsum('qkgd,pkd->kgqp', query_block, key_rows, precision=PRECISE) * score_scale)
        visible = (seg_block[:, None] == segment[None, :]) & (place_block[:, None] >= places[None, :])
        scores = jnp.where(visible[None, None], scores, MASKED)
        row_max = lax.optimization_barrier(jnp.max(scores, -1, keepdims=True))
        exponent = jnp.exp(scores - row_max)
        shares = low(exponent / lax.optimization_barrier(jnp.sum(exponent, -1, keepdims=True)))
        mixed_rows = jnp.einsum('kgqp,pkd->qkgd', shares, value_rows, precision=PRECISE)
        return mixed_rows.reshape(block_len, HEADS * HD)
    mixed_rows = lax.map(jax.checkpoint(one_block), (queries.reshape(block_count, block_len, KV, groups, HD), segment.reshape(block_count, block_len), places.reshape(block_count, block_len)))
    return mixed_rows.reshape(length, HEADS * HD)

def layer(hidden, gain_pair, qkv_weight, out_weight, gate_up_weight, down_weight, segment, docpos):
    length = hidden.shape[0]
    query_width = HEADS * HD
    kv_width = KV * HD
    normed = low(norm_scale(hidden, gain_pair[0]))
    projected = low_back(matmul(normed, qkv_weight))
    queries = low(rotate(projected[:, :query_width].reshape(length, HEADS, HD), docpos))
    key_rows = low(rotate(projected[:, query_width:query_width + kv_width].reshape(length, KV, HD), docpos))
    value_rows = low(projected[:, query_width + kv_width:].reshape(length, KV, HD))
    mixed_rows = low(low_back(attention(queries, key_rows, value_rows, segment)))
    attended = hidden + low_back(matmul(mixed_rows, out_weight))
    normed_two = low(norm_scale(attended, gain_pair[1]))
    gate_up = low_back(matmul(normed_two, gate_up_weight))
    half_width = gate_up.shape[1] // 2
    inner_rows = low(jax.nn.silu(gate_up[:, :half_width]) * gate_up[:, half_width:])
    return attended + low_back(matmul(inner_rows, down_weight))

def reference(tokens, cotangent, doc_lengths, norm_gains, w_qkv, w_out, w_gate_up, w_down):
    row_total = MB * (ROWS // PACK)
    inputs = tokens.astype(jnp.float32).reshape(row_total, PACK, D)
    upstream = cotangent.astype(jnp.float32).reshape(row_total, PACK, D)
    lengths = doc_lengths.reshape(row_total, 3)
    segment, docpos = lax.map(lambda row_lengths: layout(row_lengths, PACK), lengths)
    gains_f = norm_gains.astype(jnp.float32)
    qkv_f = w_qkv.astype(jnp.float32)
    out_f = w_out.astype(jnp.float32)
    gate_up_f = w_gate_up.astype(jnp.float32)
    down_f = w_down.astype(jnp.float32)

    def forward(first_inputs, tap_rows, gain_all, qkv_all, out_all, gate_up_all, down_all):

        def one_pack(operands):
            first_input, tap_row, seg_rows, pos_rows = operands
            first_out = layer(first_input, gain_all[0], qkv_all[0], out_all[0], gate_up_all[0], down_all[0], seg_rows, pos_rows)
            second_in = low_back(low(first_out)) + tap_row
            second_out = layer(second_in, gain_all[1], qkv_all[1], out_all[1], gate_up_all[1], down_all[1], seg_rows, pos_rows)
            return (first_out, second_out)
        return lax.map(jax.checkpoint(one_pack), (first_inputs, tap_rows, segment, docpos))
    tap_rows = jnp.zeros_like(inputs)
    outputs, pullback = jax.vjp(forward, inputs, tap_rows, gains_f, qkv_f, out_f, gate_up_f, down_f)
    first_out, second_out = outputs
    gradients = pullback((jnp.zeros_like(first_out), upstream))
    input_grad, tap_grad, grad_gains, grad_qkv, grad_out, grad_gate_up, grad_down = gradients
    activations = jnp.stack([first_out.reshape(MB, ROWS, D), second_out.reshape(MB, ROWS, D)]).astype(jnp.bfloat16)
    input_grads = jnp.stack([input_grad.reshape(MB, ROWS, D), tap_grad.reshape(MB, ROWS, D)])
    return (activations, input_grads, grad_gains[:, 0], grad_gains[:, 1], grad_qkv, grad_out, grad_gate_up, grad_down)
```

```python
from functools import partial

import jax
import jax.numpy as jnp
from jax import lax
from jax.experimental import pallas as pl
from jax.experimental.pallas import tpu as pltpu
from jax.sharding import PartitionSpec as P

HEADS = 9
KV = 3
HD = 64
PACK = 1024


EPSILON = 1e-05
ROPE_BASE = 100000.0
MASKED = -1e30


def shifted(value, axis, steps):
    count = lax.axis_size(axis)
    leading, last = (max(0, -steps), min(count, count - steps))
    return lax.ppermute(value, axis, [(source, source + steps) for source in range(leading, last)])


def matmul(left_side, right_side):
    return jnp.dot(left_side, right_side, preferred_element_type=jnp.float32)


def times_transposed(left_side, right_side):
    return lax.dot_general(
        left_side, right_side, (((1,), (1,)), ((), ())), preferred_element_type=jnp.float32
    )


def transposed_times(left_side, right_side):
    return lax.dot_general(
        left_side, right_side, (((0,), (0,)), ((), ())), preferred_element_type=jnp.float32
    )


def norm_scale(values, norm_gain):
    return values * lax.rsqrt(jnp.mean(values * values, -1, keepdims=True) + EPSILON) * norm_gain


def swiglu(gate_up):
    half_width = gate_up.shape[1] // 2
    return jax.nn.silu(gate_up[:, :half_width]) * gate_up[:, half_width:]


def rotate(values, docpos):
    half_size = values.shape[-1] // 2
    frequency = ROPE_BASE ** (-(jnp.arange(half_size, dtype=jnp.float32) * 2.0 / values.shape[-1]))
    angles = docpos[:, None] * frequency[None, :]
    cosine = jnp.cos(angles)[:, None, :]
    sine_rows = jnp.sin(angles)[:, None, :]
    lower_half = values[..., :half_size]
    upper_half = values[..., half_size:]
    return jnp.concatenate(
        [
            lower_half * cosine - upper_half * sine_rows,
            upper_half * cosine + lower_half * sine_rows,
        ],
        -1,
    )


def rotate_back(grads, docpos):
    _, pullback = jax.vjp(partial(rotate, docpos=docpos), jnp.zeros(grads.shape, jnp.float32))
    return pullback(grads)[0]


def layout(lengths, pack_len):
    seq_ends = jnp.cumsum(lengths)
    starts = seq_ends - lengths
    places = jnp.arange(pack_len, dtype=jnp.int32)
    segment = jnp.sum((places[:, None] >= seq_ends[None, :2]).astype(jnp.int32), -1)
    owners = segment[:, None] == jnp.arange(3, dtype=jnp.int32)[None, :]
    begins = jnp.sum(jnp.where(owners, starts[None, :], 0), -1)
    docpos = (places - begins).astype(jnp.float32)
    return (segment, docpos)


MESH = pl.DeviceIdType.MESH
VMEM_LIMIT = 56 * 1024 * 1024


def flip(index, bit):
    return index + bit * (1 - 2 * ((index // bit) % 2))


def bits_of(count):
    bit, found = 1, []
    while bit < count:
        found.append(bit)
        bit *= 2
    return found


def meet(fsdp_me, ctx_me, fsdp_count, ctx_count):
    barrier = pltpu.get_barrier_semaphore()
    for bit in bits_of(fsdp_count):
        pl.semaphore_signal(
            barrier, inc=1, device_id={"fsdp": flip(fsdp_me, bit)}, device_id_type=MESH
        )
    for step in range(1, ctx_count):
        pl.semaphore_signal(
            barrier, inc=1, device_id={"ctx": (ctx_me + step) % ctx_count}, device_id_type=MESH
        )
    pl.semaphore_wait(barrier, len(bits_of(fsdp_count)) + ctx_count - 1)


def gather_kernel(fsdp_count, ctx_count, chunk_count, *refs):
    shards = refs[:chunk_count]
    fulls = refs[chunk_count : 2 * chunk_count]
    local_sem, send_sem, recv_sem = refs[2 * chunk_count :]
    fsdp_me, ctx_me = lax.axis_index("fsdp"), lax.axis_index("ctx")
    bits = bits_of(fsdp_count)[::-1]
    stage_count = 1 + len(bits)

    def copies(chunk, stage):
        full = fulls[chunk]
        if stage == 0:
            return [
                pltpu.make_async_remote_copy(
                    src_ref=shards[chunk],
                    dst_ref=full.at[fsdp_me, ctx_me],
                    send_sem=send_sem.at[chunk, step - 1],
                    recv_sem=recv_sem.at[chunk, step - 1],
                    device_id={"ctx": (ctx_me + step) % ctx_count},
                    device_id_type=MESH,
                )
                for step in range(1, ctx_count)
            ]
        bit = bits[stage - 1]
        first = ctx_count - 1 + sum(fsdp_count // (2 * other) for other in bits[: stage - 1])
        made = []
        for high in range(fsdp_count // (2 * bit)):
            run = fsdp_me % (2 * bit) + high * 2 * bit
            made.append(
                pltpu.make_async_remote_copy(
                    src_ref=full.at[run],
                    dst_ref=full.at[run],
                    send_sem=send_sem.at[chunk, first + high],
                    recv_sem=recv_sem.at[chunk, first + high],
                    device_id={"fsdp": flip(fsdp_me, bit)},
                    device_id_type=MESH,
                )
            )
        return made

    own = [
        pltpu.make_async_copy(
            shards[chunk], fulls[chunk].at[fsdp_me, ctx_me], local_sem.at[chunk]
        )
        for chunk in range(chunk_count)
    ]
    for copy in own:
        copy.start()
    meet(fsdp_me, ctx_me, fsdp_count, ctx_count)
    for turn in range(chunk_count + stage_count):
        for chunk in range(chunk_count):
            stage = turn - chunk
            if stage < 0 or stage > stage_count:
                continue
            if stage == 1:
                own[chunk].wait()
            if stage >= 1:
                for copy in copies(chunk, stage - 1):
                    copy.wait_recv()
            if stage < stage_count:
                for copy in copies(chunk, stage):
                    copy.start()
    for chunk in range(chunk_count):
        for stage in range(stage_count):
            for copy in copies(chunk, stage):
                copy.wait_send()


def gather_shards(shards, fsdp_count, ctx_count):
    chunk_count = len(shards)
    slots = ctx_count - 1 + fsdp_count - 1
    return pl.pallas_call(
        partial(gather_kernel, fsdp_count, ctx_count, chunk_count),
        out_shape=[
            jax.ShapeDtypeStruct((fsdp_count, ctx_count) + shard.shape, shard.dtype)
            for shard in shards
        ],
        in_specs=[pl.BlockSpec(memory_space=pl.ANY)] * chunk_count,
        out_specs=[pl.BlockSpec(memory_space=pl.ANY)] * chunk_count,
        scratch_shapes=[
            pltpu.SemaphoreType.DMA((chunk_count,)),
            pltpu.SemaphoreType.DMA((chunk_count, slots)),
            pltpu.SemaphoreType.DMA((chunk_count, slots)),
        ],
        compiler_params=pltpu.CompilerParams(collective_id=0, has_side_effects=True),
        name="gather_weights",
    )(*shards)


def reduce_kernel(fsdp_count, ctx_count, chunk_count, *refs):
    bits = bits_of(fsdp_count)
    level_count = len(bits)
    parts = refs[:chunk_count]
    outs = refs[chunk_count : 2 * chunk_count]
    scratch = refs[2 * chunk_count :]
    per_chunk = 2 * level_count + 1
    send_sem, recv_sem = scratch[chunk_count * per_chunk :]
    fsdp_me, ctx_me = lax.axis_index("fsdp"), lax.axis_index("ctx")

    def level(chunk, index):
        return parts[chunk] if index == 0 else scratch[chunk * per_chunk + 2 * index - 1]

    def landing(chunk, index):
        return scratch[chunk * per_chunk + 2 * index]

    def copies(chunk, stage):
        source = level(chunk, stage)
        if stage == level_count:
            return [
                pltpu.make_async_remote_copy(
                    src_ref=source.at[0, (ctx_me + step) % ctx_count],
                    dst_ref=landing(chunk, stage).at[step - 1],
                    send_sem=send_sem.at[chunk, fsdp_count - 1 + step - 1],
                    recv_sem=recv_sem.at[chunk, fsdp_count - 1 + step - 1],
                    device_id={"ctx": (ctx_me + step) % ctx_count},
                    device_id_type=MESH,
                )
                for step in range(1, ctx_count)
            ]
        bit = bits[stage]
        first = sum(fsdp_count // (2 * other) for other in bits[:stage])
        mine = (fsdp_me // bit) % 2
        return [
            pltpu.make_async_remote_copy(
                src_ref=source.at[1 - mine + 2 * high],
                dst_ref=landing(chunk, stage).at[high],
                send_sem=send_sem.at[chunk, first + high],
                recv_sem=recv_sem.at[chunk, first + high],
                device_id={"fsdp": flip(fsdp_me, bit)},
                device_id_type=MESH,
            )
            for high in range(fsdp_count // (2 * bit))
        ]

    def absorb(chunk, stage):
        source, landed = level(chunk, stage), landing(chunk, stage)
        if stage == level_count:
            total = source[0, ctx_me].astype(jnp.float32)
            for step in range(1, ctx_count):
                total = total + landed[step - 1].astype(jnp.float32)
            outs[chunk][...] = total
            return
        mine = (fsdp_me // bits[stage]) % 2
        target = level(chunk, stage + 1)
        for high in range(fsdp_count // (2 * bits[stage])):

            def add(place, carry):
                total = source[mine + 2 * high, place].astype(jnp.float32) + landed[
                    high, place
                ].astype(jnp.float32)
                target[high, place] = total.astype(jnp.bfloat16)
                return carry

            lax.fori_loop(0, ctx_count, add, 0)

    meet(fsdp_me, ctx_me, fsdp_count, ctx_count)
    for turn in range(chunk_count + level_count + 1):
        for chunk in range(chunk_count):
            stage = turn - chunk
            if stage < 0 or stage > level_count + 1:
                continue
            if stage >= 1:
                for copy in copies(chunk, stage - 1):
                    copy.wait_recv()
                absorb(chunk, stage - 1)
            if stage <= level_count:
                for copy in copies(chunk, stage):
                    copy.start()
    for chunk in range(chunk_count):
        for stage in range(level_count + 1):
            for copy in copies(chunk, stage):
                copy.wait_send()


def reduce_parts(parts, fsdp_count, ctx_count):
    chunk_count = len(parts)
    slots = ctx_count - 1 + fsdp_count - 1
    scratch = []
    for part in parts:
        shard = part.shape[2:]
        for bit in bits_of(fsdp_count):
            half = (fsdp_count // (2 * bit), ctx_count) + shard
            scratch += [pltpu.VMEM(half, jnp.bfloat16), pltpu.VMEM(half, jnp.bfloat16)]
        scratch.append(pltpu.VMEM((ctx_count - 1,) + shard, jnp.bfloat16))
    return pl.pallas_call(
        partial(reduce_kernel, fsdp_count, ctx_count, chunk_count),
        out_shape=[jax.ShapeDtypeStruct(part.shape[2:], jnp.float32) for part in parts],
        in_specs=[pl.BlockSpec(memory_space=pltpu.VMEM)] * chunk_count,
        out_specs=[pl.BlockSpec(memory_space=pltpu.VMEM)] * chunk_count,
        scratch_shapes=scratch
        + [
            pltpu.SemaphoreType.DMA((chunk_count, slots)),
            pltpu.SemaphoreType.DMA((chunk_count, slots)),
        ],
        compiler_params=pltpu.CompilerParams(
            collective_id=1, has_side_effects=True, vmem_limit_bytes=VMEM_LIMIT
        ),
        name="reduce_grads",
    )(*parts)


def visible_pairs(seg_q_ref, seg_k_ref, place_ref):
    seg_q, seg_k = seg_q_ref[...], seg_k_ref[...]
    columns = lax.broadcasted_iota(jnp.int32, (seg_q.shape[0], seg_k.shape[1]), 1)
    return (seg_q == seg_k) & (place_ref[...] >= columns)


def attend_kernel(q_ref, k_ref, v_ref, seg_q_ref, seg_k_ref, place_ref, o_ref):
    visible = visible_pairs(seg_q_ref, seg_k_ref, place_ref)
    for head in range(q_ref.shape[0]):
        scores = times_transposed(q_ref[head], k_ref[...]) * HD ** (-0.5)
        scores = jnp.where(visible, scores, MASKED)
        exponent = jnp.exp(scores - jnp.max(scores, -1, keepdims=True))
        shares = exponent * (1.0 / jnp.sum(exponent, -1, keepdims=True))
        o_ref[head] = matmul(shares.astype(jnp.bfloat16), v_ref[...]).astype(jnp.bfloat16)


def attend_back_kernel(
    q_ref, k_ref, v_ref, go_ref, seg_q_ref, seg_k_ref, place_ref, gq_ref, gk_ref, gv_ref
):
    visible = visible_pairs(seg_q_ref, seg_k_ref, place_ref)
    key_total, value_total = None, None
    for head in range(q_ref.shape[0]):
        scores = times_transposed(q_ref[head], k_ref[...]) * HD ** (-0.5)
        scores = jnp.where(visible, scores, MASKED)
        exponent = jnp.exp(scores - jnp.max(scores, -1, keepdims=True))
        shares = exponent * (1.0 / jnp.sum(exponent, -1, keepdims=True))
        share_grad = times_transposed(go_ref[head], v_ref[...])
        row_dot = jnp.sum(shares * share_grad, -1, keepdims=True)
        score_grad = (shares * (share_grad - row_dot)).astype(jnp.bfloat16)
        gq_ref[head] = matmul(score_grad, k_ref[...]) * HD ** (-0.5)
        key_part = transposed_times(score_grad, q_ref[head])
        value_part = transposed_times(shares.astype(jnp.bfloat16), go_ref[head])
        key_total = key_part if key_total is None else key_total + key_part
        value_total = value_part if value_total is None else value_total + value_part
    gk_ref[...] = (key_total * HD ** (-0.5)).astype(jnp.bfloat16)
    gv_ref[...] = value_total.astype(jnp.bfloat16)


def attention_call(kernel, operands, masks, outs, name):
    micro_count, kv_count = operands[0].shape[:2]

    def spec(shape):
        rank = len(shape) - 2
        return pl.BlockSpec(
            (None, None) + tuple(shape[2:]), lambda micro, group: (micro, group) + (0,) * rank
        )

    seg_q, seg_k, place = masks
    return pl.pallas_call(
        kernel,
        grid=(micro_count, kv_count),
        out_shape=[jax.ShapeDtypeStruct(shape, kind) for shape, kind in outs],
        in_specs=[spec(operand.shape) for operand in operands]
        + [
            pl.BlockSpec((None,) + seg_q.shape[1:], lambda micro, group: (micro, 0, 0)),
            pl.BlockSpec((None,) + seg_k.shape[1:], lambda micro, group: (micro, 0, 0)),
            pl.BlockSpec(place.shape, lambda micro, group: (0, 0)),
        ],
        out_specs=[spec(shape) for shape, kind in outs],
        compiler_params=pltpu.CompilerParams(vmem_limit_bytes=VMEM_LIMIT),
        name=name,
    )(*operands, *masks)


def group_heads(values, micro_count):
    rows = values.reshape(micro_count, -1, KV, HEADS // KV, HD)
    return jnp.transpose(rows, (0, 2, 3, 1, 4))


def split_keys(pack_kv, micro_count):
    halves = pack_kv.reshape(micro_count, -1, 2, KV, HD)
    halves = jnp.transpose(halves, (2, 0, 3, 1, 4))
    return halves[0], halves[1]


def layer_forward(hidden_in, masks, local_pos, weights, micro_count):
    gain_pair, qkv_weight, out_weight, gate_up_weight, down_weight = weights
    row_count = hidden_in.shape[0]
    query_width = HEADS * HD
    kv_width = KV * HD
    hidden = hidden_in.astype(jnp.float32)
    normed = norm_scale(hidden, gain_pair[0]).astype(jnp.bfloat16)
    projected = matmul(normed, qkv_weight)
    queries = rotate(projected[:, :query_width].reshape(row_count, HEADS, HD), local_pos).astype(
        jnp.bfloat16
    )
    key_part = rotate(
        projected[:, query_width : query_width + kv_width].reshape(row_count, KV, HD), local_pos
    )
    local_kv = jnp.concatenate(
        [key_part.reshape(row_count, kv_width), projected[:, query_width + kv_width :]], -1
    ).astype(jnp.bfloat16)
    pack_kv = lax.all_gather(
        local_kv.reshape(micro_count, -1, 2 * kv_width), "ctx", axis=1, tiled=True
    )
    query_groups = group_heads(queries, micro_count)
    key_groups, value_groups = split_keys(pack_kv, micro_count)
    mixed_groups = attention_call(
        attend_kernel,
        (query_groups, key_groups, value_groups),
        masks,
        [(query_groups.shape, jnp.bfloat16)],
        "attend",
    )[0]
    mixed_low = jnp.transpose(mixed_groups, (0, 3, 1, 2, 4)).reshape(row_count, query_width)
    attended = hidden + matmul(mixed_low, out_weight)
    normed_two = norm_scale(attended, gain_pair[1]).astype(jnp.bfloat16)
    gate_up = matmul(normed_two, gate_up_weight)
    inner_rows = swiglu(gate_up).astype(jnp.bfloat16)
    result = (attended + matmul(inner_rows, down_weight)).astype(jnp.bfloat16)
    saved = (
        hidden,
        normed,
        (query_groups, key_groups, value_groups),
        mixed_low,
        attended,
        normed_two,
        gate_up,
        inner_rows,
    )
    return (result, saved)


def layer_backward(upstream, saved, masks, local_pos, weights, micro_count):
    gain_pair, qkv_weight, out_weight, gate_up_weight, down_weight = weights
    hidden, normed, groups, mixed_low, attended, normed_two, gate_up, inner_rows = saved
    row_count = hidden.shape[0]
    kv_width = KV * HD
    branch_grad = upstream.astype(jnp.bfloat16)
    inner_grad = times_transposed(branch_grad, down_weight)
    gate_up_grad = jax.vjp(swiglu, gate_up)[1](inner_grad)[0].astype(jnp.bfloat16)
    normed_two_grad = times_transposed(gate_up_grad, gate_up_weight)
    _, pull_two = jax.vjp(norm_scale, attended, gain_pair[1])
    attended_part, gain_two_grad = pull_two(normed_two_grad)
    attended_grad = upstream + attended_part
    out_branch = attended_grad.astype(jnp.bfloat16)
    mixed_grad = times_transposed(out_branch, out_weight).astype(jnp.bfloat16)
    query_groups, key_groups, value_groups = groups
    query_grad, key_grad, value_grad = attention_call(
        attend_back_kernel,
        (query_groups, key_groups, value_groups, group_heads(mixed_grad, micro_count)),
        masks,
        [
            (query_groups.shape, jnp.float32),
            (key_groups.shape, jnp.bfloat16),
            (value_groups.shape, jnp.bfloat16),
        ],
        "attend_back",
    )
    query_grad = jnp.transpose(query_grad, (0, 3, 1, 2, 4)).reshape(row_count, HEADS, HD)
    pack_kv_grad = jnp.transpose(jnp.stack([key_grad, value_grad]), (1, 3, 0, 2, 4))
    pack_kv_grad = pack_kv_grad.reshape(micro_count, -1, 2 * kv_width)
    local_kv_grad = (
        lax.psum_scatter(pack_kv_grad, "ctx", scatter_dimension=1, tiled=True)
        .astype(jnp.float32)
        .reshape(row_count, 2 * kv_width)
    )
    query_pre = rotate_back(query_grad, local_pos).reshape(row_count, HEADS * HD)
    key_pre = rotate_back(
        local_kv_grad[:, :kv_width].reshape(row_count, KV, HD), local_pos
    ).reshape(row_count, kv_width)
    projected_grad = jnp.concatenate([query_pre, key_pre, local_kv_grad[:, kv_width:]], -1).astype(
        jnp.bfloat16
    )
    normed_grad = times_transposed(projected_grad, qkv_weight)
    _, pull_one = jax.vjp(norm_scale, hidden, gain_pair[0])
    hidden_part, gain_one_grad = pull_one(normed_grad)
    input_grad = attended_grad + hidden_part

    def weight_grads():
        return (
            gain_one_grad,
            gain_two_grad,
            transposed_times(normed, projected_grad),
            transposed_times(mixed_low, out_branch),
            transposed_times(normed_two, gate_up_grad),
            transposed_times(inner_rows, branch_grad),
        )

    return (input_grad, weight_grads)


def on_device(tokens, cotangent, doc_lengths, norm_gains, w_qkv, w_out, w_gate_up, w_down):
    section_index = lax.axis_index("section")
    ctx_index = lax.axis_index("ctx")
    fsdp_count, ctx_count = lax.axis_size("fsdp"), lax.axis_size("ctx")
    micro_count, token_count, width = tokens.shape
    row_count = micro_count * token_count
    qkv_width = w_qkv.shape[2]
    half_ff = w_gate_up.shape[2] // 2
    spare = -(qkv_width + 2) % 128
    first_shard = jnp.concatenate(
        [w_qkv[0], norm_gains[0].T, jnp.zeros((w_qkv.shape[1], spare), jnp.bfloat16)], -1
    )
    shards = (
        first_shard,
        w_out[0],
        w_gate_up[0, :, :half_ff],
        w_gate_up[0, :, half_ff:],
        w_down[0],
    )
    fulls = gather_shards(shards, fsdp_count, ctx_count)
    fulls = [full.reshape(-1, full.shape[-1]) for full in fulls]
    gain_pair = fulls[0][:, qkv_width : qkv_width + 2].T.astype(jnp.float32)
    weights = (
        gain_pair,
        fulls[0][:, :qkv_width],
        fulls[1],
        jnp.concatenate([fulls[2], fulls[3]], -1),
        fulls[4],
    )
    offset = ctx_index * token_count
    seg_k, pos_k = jax.vmap(lambda lengths: layout(lengths, PACK))(doc_lengths[:, 0])
    seg_q = lax.dynamic_slice_in_dim(seg_k, offset, token_count, 1)
    local_pos = lax.dynamic_slice_in_dim(pos_k, offset, token_count, 1).reshape(row_count)
    place = offset + jnp.arange(token_count, dtype=jnp.int32)
    masks = (seg_q[:, :, None], seg_k[:, None, :], place[:, None])

    first_input = tokens.reshape(row_count, width)
    first_result, _ = layer_forward(first_input, masks, local_pos, weights, micro_count)
    incoming = shifted(first_result, "section", 1)
    hidden_in = jnp.where(section_index == 0, first_input, incoming)
    result, saved = layer_forward(hidden_in, masks, local_pos, weights, micro_count)
    given = cotangent.reshape(row_count, width).astype(jnp.float32)
    last_grad, _ = layer_backward(given, saved, masks, local_pos, weights, micro_count)
    incoming_grad = shifted(last_grad.astype(jnp.bfloat16), "section", -1)
    upstream = jnp.where(section_index == 1, given, incoming_grad.astype(jnp.float32))
    input_grad, weight_grads = layer_backward(
        upstream, saved, masks, local_pos, weights, micro_count
    )
    gain_one, gain_two, grad_qkv, grad_out, grad_gate_up, grad_down = weight_grads()
    spare_columns = jnp.zeros((width, spare), jnp.float32)
    first_grad = jnp.concatenate(
        [grad_qkv, gain_one[:, None], gain_two[:, None], spare_columns], -1
    )
    parts = (
        first_grad,
        grad_out,
        grad_gate_up[:, :half_ff],
        grad_gate_up[:, half_ff:],
        grad_down,
    )
    parts = [
        part.astype(jnp.bfloat16).reshape(fsdp_count, ctx_count, -1, part.shape[-1])
        for part in parts
    ]
    totals = reduce_parts(parts, fsdp_count, ctx_count)
    shape = (1, micro_count, token_count, width)
    return (
        result.reshape(shape),
        input_grad.reshape(shape),
        totals[0][None, :, qkv_width],
        totals[0][None, :, qkv_width + 1],
        totals[0][None, :, :qkv_width],
        totals[1][None],
        jnp.concatenate([totals[2], totals[3]], -1)[None],
        totals[4][None],
    )


def solution(mesh):
    return jax.shard_map(
        on_device,
        mesh=mesh,
        in_specs=(
            P(None, ("fsdp", "ctx"), None),
            P(None, ("fsdp", "ctx"), None),
            P(None, "fsdp", None),
            P("section", None, ("fsdp", "ctx")),
            P("section", ("fsdp", "ctx"), None),
            P("section", ("fsdp", "ctx"), None),
            P("section", ("fsdp", "ctx"), None),
            P("section", ("fsdp", "ctx"), None),
        ),
        out_specs=(
            P("section", None, ("fsdp", "ctx"), None),
            P("section", None, ("fsdp", "ctx"), None),
            P("section", ("fsdp", "ctx")),
            P("section", ("fsdp", "ctx")),
            P("section", ("fsdp", "ctx"), None),
            P("section", ("fsdp", "ctx"), None),
            P("section", ("fsdp", "ctx"), None),
            P("section", ("fsdp", "ctx"), None),
        ),
        check_vma=False,
    )
```

```python
from functools import partial

import jax
import jax.numpy as jnp
from jax import lax
from jax.experimental import pallas as pl
from jax.experimental.pallas import tpu as pltpu
from jax.sharding import PartitionSpec as P

HEADS = 9
KV = 3
HD = 64
PACK = 1024


EPSILON = 1e-05
ROPE_BASE = 100000.0
MASKED = -1e30


def shifted(value, axis, steps):
    count = lax.axis_size(axis)
    leading, last = (max(0, -steps), min(count, count - steps))
    return lax.ppermute(value, axis, [(source, source + steps) for source in range(leading, last)])


def matmul(left_side, right_side):
    return jnp.dot(left_side, right_side, preferred_element_type=jnp.float32)


def times_transposed(left_side, right_side):
    return lax.dot_general(
        left_side, right_side, (((1,), (1,)), ((), ())), preferred_element_type=jnp.float32
    )


def transposed_times(left_side, right_side):
    return lax.dot_general(
        left_side, right_side, (((0,), (0,)), ((), ())), preferred_element_type=jnp.float32
    )


def norm_scale(values, norm_gain):
    return values * lax.rsqrt(jnp.mean(values * values, -1, keepdims=True) + EPSILON) * norm_gain


def swiglu(gate_up):
    half_width = gate_up.shape[1] // 2
    return jax.nn.silu(gate_up[:, :half_width]) * gate_up[:, half_width:]


def layout(lengths, pack_len):
    seq_ends = jnp.cumsum(lengths)
    starts = seq_ends - lengths
    places = jnp.arange(pack_len, dtype=jnp.int32)
    segment = jnp.sum((places[:, None] >= seq_ends[None, :2]).astype(jnp.int32), -1)
    owners = segment[:, None] == jnp.arange(3, dtype=jnp.int32)[None, :]
    begins = jnp.sum(jnp.where(owners, starts[None, :], 0), -1)
    docpos = (places - begins).astype(jnp.float32)
    return (segment, docpos)


MESH = pl.DeviceIdType.MESH
VMEM_LIMIT = 56 * 1024 * 1024


def flip(index, bit):
    return index + bit * (1 - 2 * ((index // bit) % 2))


def bits_of(count):
    bit, found = 1, []
    while bit < count:
        found.append(bit)
        bit *= 2
    return found


def meet(fsdp_me, ctx_me, fsdp_count, ctx_count):
    barrier = pltpu.get_barrier_semaphore()
    for bit in bits_of(fsdp_count):
        pl.semaphore_signal(
            barrier, inc=1, device_id={"fsdp": flip(fsdp_me, bit)}, device_id_type=MESH
        )
    for step in range(1, ctx_count):
        pl.semaphore_signal(
            barrier, inc=1, device_id={"ctx": (ctx_me + step) % ctx_count}, device_id_type=MESH
        )
    pl.semaphore_wait(barrier, len(bits_of(fsdp_count)) + ctx_count - 1)


def gather_kernel(fsdp_count, ctx_count, chunk_count, *refs):
    shards = refs[:chunk_count]
    fulls = refs[chunk_count : 2 * chunk_count]
    local_sem, send_sem, recv_sem = refs[2 * chunk_count :]
    fsdp_me, ctx_me = lax.axis_index("fsdp"), lax.axis_index("ctx")
    bits = bits_of(fsdp_count)[::-1]
    stage_count = 1 + len(bits)

    def copies(chunk, stage):
        full = fulls[chunk]
        if stage == 0:
            return [
                pltpu.make_async_remote_copy(
                    src_ref=shards[chunk],
                    dst_ref=full.at[fsdp_me, ctx_me],
                    send_sem=send_sem.at[chunk, step - 1],
                    recv_sem=recv_sem.at[chunk, step - 1],
                    device_id={"ctx": (ctx_me + step) % ctx_count},
                    device_id_type=MESH,
                )
                for step in range(1, ctx_count)
            ]
        bit = bits[stage - 1]
        first = ctx_count - 1 + sum(fsdp_count // (2 * other) for other in bits[: stage - 1])
        made = []
        for high in range(fsdp_count // (2 * bit)):
            run = fsdp_me % (2 * bit) + high * 2 * bit
            made.append(
                pltpu.make_async_remote_copy(
                    src_ref=full.at[run],
                    dst_ref=full.at[run],
                    send_sem=send_sem.at[chunk, first + high],
                    recv_sem=recv_sem.at[chunk, first + high],
                    device_id={"fsdp": flip(fsdp_me, bit)},
                    device_id_type=MESH,
                )
            )
        return made

    own = [
        pltpu.make_async_copy(
            shards[chunk], fulls[chunk].at[fsdp_me, ctx_me], local_sem.at[chunk]
        )
        for chunk in range(chunk_count)
    ]
    for copy in own:
        copy.start()
    meet(fsdp_me, ctx_me, fsdp_count, ctx_count)
    for chunk in range(chunk_count):
        for copy in copies(chunk, 0):
            copy.start()
    for turn in range(chunk_count + stage_count):
        for chunk in range(chunk_count):
            stage = turn - chunk
            if stage < 1 or stage > stage_count:
                continue
            if stage == 1:
                own[chunk].wait()
            if stage >= 1:
                for copy in copies(chunk, stage - 1):
                    copy.wait_recv()
            if stage < stage_count:
                for copy in copies(chunk, stage):
                    copy.start()
    for chunk in range(chunk_count):
        for stage in range(stage_count):
            for copy in copies(chunk, stage):
                copy.wait_send()


def gather_shards(shards, fsdp_count, ctx_count):
    chunk_count = len(shards)
    slots = ctx_count - 1 + fsdp_count - 1
    return pl.pallas_call(
        partial(gather_kernel, fsdp_count, ctx_count, chunk_count),
        out_shape=[
            jax.ShapeDtypeStruct((fsdp_count, ctx_count) + shard.shape, shard.dtype)
            for shard in shards
        ],
        in_specs=[pl.BlockSpec(memory_space=pl.ANY)] * chunk_count,
        out_specs=[pl.BlockSpec(memory_space=pl.ANY)] * chunk_count,
        scratch_shapes=[
            pltpu.SemaphoreType.DMA((chunk_count,)),
            pltpu.SemaphoreType.DMA((chunk_count, slots)),
            pltpu.SemaphoreType.DMA((chunk_count, slots)),
        ],
        compiler_params=pltpu.CompilerParams(collective_id=0, has_side_effects=True),
        name="gather_weights",
    )(*shards)


def reduce_kernel(fsdp_count, ctx_count, chunk_count, *refs):
    bits = bits_of(fsdp_count)
    level_count = len(bits)
    parts = refs[:chunk_count]
    outs = refs[chunk_count : 2 * chunk_count]
    scratch = refs[2 * chunk_count :]
    per_chunk = 2 * level_count + 1
    send_sem, recv_sem = scratch[chunk_count * per_chunk :]
    fsdp_me, ctx_me = lax.axis_index("fsdp"), lax.axis_index("ctx")

    def level(chunk, index):
        return parts[chunk] if index == 0 else scratch[chunk * per_chunk + 2 * index - 1]

    def landing(chunk, index):
        return scratch[chunk * per_chunk + 2 * index]

    def copies(chunk, stage):
        source = level(chunk, stage)
        if stage == level_count:
            return [
                pltpu.make_async_remote_copy(
                    src_ref=source.at[0, (ctx_me + step) % ctx_count],
                    dst_ref=landing(chunk, stage).at[step - 1],
                    send_sem=send_sem.at[chunk, fsdp_count - 1 + step - 1],
                    recv_sem=recv_sem.at[chunk, fsdp_count - 1 + step - 1],
                    device_id={"ctx": (ctx_me + step) % ctx_count},
                    device_id_type=MESH,
                )
                for step in range(1, ctx_count)
            ]
        bit = bits[stage]
        first = sum(fsdp_count // (2 * other) for other in bits[:stage])
        mine = (fsdp_me // bit) % 2
        return [
            pltpu.make_async_remote_copy(
                src_ref=source.at[1 - mine + 2 * high],
                dst_ref=landing(chunk, stage).at[high],
                send_sem=send_sem.at[chunk, first + high],
                recv_sem=recv_sem.at[chunk, first + high],
                device_id={"fsdp": flip(fsdp_me, bit)},
                device_id_type=MESH,
            )
            for high in range(fsdp_count // (2 * bit))
        ]

    def absorb(chunk, stage):
        source, landed = level(chunk, stage), landing(chunk, stage)
        if stage == level_count:
            total = source[0, ctx_me].astype(jnp.float32)
            for step in range(1, ctx_count):
                total = total + landed[step - 1].astype(jnp.float32)
            outs[chunk][...] = total
            return
        mine = (fsdp_me // bits[stage]) % 2
        target = level(chunk, stage + 1)
        for high in range(fsdp_count // (2 * bits[stage])):

            def add(place, carry):
                total = source[mine + 2 * high, place].astype(jnp.float32) + landed[
                    high, place
                ].astype(jnp.float32)
                target[high, place] = total.astype(jnp.bfloat16)
                return carry

            lax.fori_loop(0, ctx_count, add, 0)

    meet(fsdp_me, ctx_me, fsdp_count, ctx_count)
    for chunk in range(chunk_count):
        for copy in copies(chunk, 0):
            copy.start()
    for turn in range(chunk_count + level_count + 1):
        for chunk in range(chunk_count):
            stage = turn - chunk
            if stage < 1 or stage > level_count + 1:
                continue
            for copy in copies(chunk, stage - 1):
                copy.wait_recv()
            absorb(chunk, stage - 1)
            if stage <= level_count:
                for copy in copies(chunk, stage):
                    copy.start()
    for chunk in range(chunk_count):
        for stage in range(level_count + 1):
            for copy in copies(chunk, stage):
                copy.wait_send()


def reduce_parts(parts, fsdp_count, ctx_count):
    chunk_count = len(parts)
    slots = ctx_count - 1 + fsdp_count - 1
    scratch = []
    for part in parts:
        shard = part.shape[2:]
        for bit in bits_of(fsdp_count):
            half = (fsdp_count // (2 * bit), ctx_count) + shard
            scratch += [pltpu.VMEM(half, jnp.bfloat16), pltpu.VMEM(half, jnp.bfloat16)]
        scratch.append(pltpu.VMEM((ctx_count - 1,) + shard, jnp.bfloat16))
    return pl.pallas_call(
        partial(reduce_kernel, fsdp_count, ctx_count, chunk_count),
        out_shape=[jax.ShapeDtypeStruct(part.shape[2:], jnp.float32) for part in parts],
        in_specs=[pl.BlockSpec(memory_space=pltpu.VMEM)] * chunk_count,
        out_specs=[pl.BlockSpec(memory_space=pltpu.VMEM)] * chunk_count,
        scratch_shapes=scratch
        + [
            pltpu.SemaphoreType.DMA((chunk_count, slots)),
            pltpu.SemaphoreType.DMA((chunk_count, slots)),
        ],
        compiler_params=pltpu.CompilerParams(
            collective_id=1, has_side_effects=True, vmem_limit_bytes=VMEM_LIMIT
        ),
        name="reduce_grads",
    )(*parts)


def visible_pairs(seg_q_ref, seg_k_ref, place_ref):
    seg_q, seg_k = seg_q_ref[...], seg_k_ref[...]
    columns = lax.broadcasted_iota(jnp.int32, (seg_q.shape[0], seg_k.shape[1]), 1)
    return (seg_q == seg_k) & (place_ref[...] >= columns)


def turned(values, cosine, signed_sine):
    lanes = lax.broadcasted_iota(jnp.int32, values.shape, 1)
    half = HD // 2
    other = jnp.where(
        lanes % HD < half,
        pltpu.roll(values, values.shape[1] - half, 1),
        pltpu.roll(values, half, 1),
    )
    return values * cosine + other * signed_sine


def project_kernel(h_ref, gain_ref, w_ref, cos_ref, sin_ref, normed_ref, q_ref, kv_ref, row_ref):
    hidden = h_ref[...].astype(jnp.float32)
    normed = norm_scale(hidden, gain_ref[...]).astype(jnp.bfloat16)
    normed_ref[...] = normed
    turned_width = (HEADS + KV) * HD
    for first in range(0, w_ref.shape[1], 128):
        block = matmul(normed, w_ref[:, first : first + 128])
        if first < turned_width:
            block = turned(block, cos_ref[...], sin_ref[...])
        row_ref[:, first : first + 128] = block
    q_ref[...] = (row_ref[:, : HEADS * HD] * HD ** (-0.5)).astype(jnp.bfloat16)
    kv_ref[...] = row_ref[:, HEADS * HD : (HEADS + 2 * KV) * HD].astype(jnp.bfloat16)


def project(hidden_in, gain, weight, cosine, signed_sine):
    rows, width = hidden_in.shape
    return pl.pallas_call(
        project_kernel,
        out_shape=[
            jax.ShapeDtypeStruct((rows, width), jnp.bfloat16),
            jax.ShapeDtypeStruct((rows, HEADS * HD), jnp.bfloat16),
            jax.ShapeDtypeStruct((rows, 2 * KV * HD), jnp.bfloat16),
        ],
        scratch_shapes=[pltpu.VMEM((rows, weight.shape[1]), jnp.float32)],
        compiler_params=pltpu.CompilerParams(vmem_limit_bytes=VMEM_LIMIT),
        name="project",
    )(hidden_in, gain, weight, cosine, signed_sine)


def unturn_kernel(gq_ref, gkv_ref, cos_ref, sin_ref, out_ref, row_ref):
    query_width = HEADS * HD
    row_ref[:, :query_width] = gq_ref[...] * HD ** (-0.5)
    row_ref[:, query_width : query_width + 2 * KV * HD] = gkv_ref[...].astype(jnp.float32)
    for first in range(0, (HEADS + KV) * HD, 128):
        block = row_ref[:, first : first + 128]
        row_ref[:, first : first + 128] = turned(block, cos_ref[...], -sin_ref[...])
    out_ref[...] = row_ref[...].astype(jnp.bfloat16)


def unturn(query_grad, kv_grad, cosine, signed_sine):
    rows = query_grad.shape[0]
    width = (HEADS + 2 * KV) * HD
    return pl.pallas_call(
        unturn_kernel,
        out_shape=jax.ShapeDtypeStruct((rows, width), jnp.bfloat16),
        scratch_shapes=[pltpu.VMEM((rows, width), jnp.float32)],
        compiler_params=pltpu.CompilerParams(vmem_limit_bytes=VMEM_LIMIT),
        name="unturn",
    )(query_grad, kv_grad, cosine, signed_sine)


def columns_of(head):
    return slice(head * HD, (head + 1) * HD)


def attend_kernel(q_ref, kv_ref, seg_q_ref, seg_k_ref, place_ref, o_ref, log_ref):
    visible = visible_pairs(seg_q_ref, seg_k_ref, place_ref)
    for head in range(HEADS):
        group = head // (HEADS // KV)
        scores = times_transposed(q_ref[:, columns_of(head)], kv_ref[:, columns_of(group)])
        scores = jnp.where(visible, scores, MASKED)
        row_max = jnp.max(scores, -1, keepdims=True)
        exponent = jnp.exp(scores - row_max)
        row_sum = jnp.sum(exponent, -1, keepdims=True)
        mixed = matmul(exponent.astype(jnp.bfloat16), kv_ref[:, columns_of(KV + group)])
        o_ref[:, columns_of(head)] = (mixed * (1.0 / row_sum)).astype(jnp.bfloat16)
        log_ref[:, head : head + 1] = row_max + jnp.log(row_sum)


def attend_back_kernel(
    q_ref, kv_ref, go_ref, log_ref, seg_q_ref, seg_k_ref, place_ref, gq_ref, gkv_ref
):
    visible = visible_pairs(seg_q_ref, seg_k_ref, place_ref)
    for group in range(KV):
        key_total, value_total = None, None
        for head in range(group * (HEADS // KV), (group + 1) * (HEADS // KV)):
            query = q_ref[:, columns_of(head)]
            grad = go_ref[:, columns_of(head)]
            keys = kv_ref[:, columns_of(group)]
            scores = times_transposed(query, keys)
            scores = jnp.where(visible, scores - log_ref[:, head : head + 1], MASKED)
            shares = jnp.exp(scores)
            share_grad = times_transposed(grad, kv_ref[:, columns_of(KV + group)])
            row_dot = jnp.sum(shares * share_grad, -1, keepdims=True)
            score_grad = (shares * (share_grad - row_dot)).astype(jnp.bfloat16)
            gq_ref[:, columns_of(head)] = matmul(score_grad, keys)
            key_part = transposed_times(score_grad, query)
            value_part = transposed_times(shares.astype(jnp.bfloat16), grad)
            key_total = key_part if key_total is None else key_total + key_part
            value_total = value_part if value_total is None else value_total + value_part
        gkv_ref[:, columns_of(group)] = key_total.astype(jnp.bfloat16)
        gkv_ref[:, columns_of(KV + group)] = value_total.astype(jnp.bfloat16)


def local_call(kernel, operands, outs, name):
    return pl.pallas_call(
        kernel,
        out_shape=[jax.ShapeDtypeStruct(shape, kind) for shape, kind in outs],
        compiler_params=pltpu.CompilerParams(vmem_limit_bytes=VMEM_LIMIT),
        cost_estimate=pl.CostEstimate(
            flops=4_000_000_000, bytes_accessed=8_000_000, transcendentals=3_000_000
        ),
        name=name,
    )(*operands)


def layer_forward(hidden_in, masks, turns, weights, micro_count):
    gain_pair, qkv_weight, out_weight, gate_up_weight, down_weight = weights
    hidden = hidden_in.astype(jnp.float32)
    normed, queries, local_kv = project(hidden_in, gain_pair[:1], qkv_weight, *turns)
    count = hidden.shape[0] // micro_count
    packs, mixed_parts, log_parts = [], [], []
    for micro in range(micro_count):
        rows = slice(micro * count, (micro + 1) * count)
        packs.append(lax.all_gather(local_kv[rows], "ctx", axis=0, tiled=True))
    for micro in range(micro_count):
        rows = slice(micro * count, (micro + 1) * count)
        mixed, logs = local_call(
            attend_kernel,
            (queries[rows], packs[micro]) + masks[micro],
            [((count, HEADS * HD), jnp.bfloat16), ((count, HEADS), jnp.float32)],
            "attend",
        )
        mixed_parts.append(mixed)
        log_parts.append(logs)
    mixed_low = jnp.concatenate(mixed_parts, 0)
    attended = hidden + matmul(mixed_low, out_weight)
    normed_two = norm_scale(attended, gain_pair[1]).astype(jnp.bfloat16)
    gate_up = matmul(normed_two, gate_up_weight)
    inner_rows = swiglu(gate_up).astype(jnp.bfloat16)
    result = (attended + matmul(inner_rows, down_weight)).astype(jnp.bfloat16)
    saved = (
        hidden,
        normed,
        (queries, packs, log_parts),
        mixed_low,
        attended,
        normed_two,
        gate_up,
        inner_rows,
    )
    return (result, saved)


def layer_backward(upstream, saved, masks, turns, weights, micro_count):
    gain_pair, qkv_weight, out_weight, gate_up_weight, down_weight = weights
    hidden, normed, parts, mixed_low, attended, normed_two, gate_up, inner_rows = saved
    count = hidden.shape[0] // micro_count
    branch_grad = upstream.astype(jnp.bfloat16)
    inner_grad = times_transposed(branch_grad, down_weight)
    gate_up_grad = jax.vjp(swiglu, gate_up)[1](inner_grad)[0].astype(jnp.bfloat16)
    normed_two_grad = times_transposed(gate_up_grad, gate_up_weight)
    _, pull_two = jax.vjp(norm_scale, attended, gain_pair[1])
    attended_part, gain_two_grad = pull_two(normed_two_grad)
    attended_grad = upstream + attended_part
    out_branch = attended_grad.astype(jnp.bfloat16)
    mixed_grad = times_transposed(out_branch, out_weight).astype(jnp.bfloat16)
    queries, packs, log_parts = parts
    query_grads, kv_grads = [], []
    for micro in range(micro_count):
        rows = slice(micro * count, (micro + 1) * count)
        query_part, kv_part = local_call(
            attend_back_kernel,
            (queries[rows], packs[micro], mixed_grad[rows], log_parts[micro]) + masks[micro],
            [((count, HEADS * HD), jnp.float32), (packs[micro].shape, jnp.bfloat16)],
            "attend_back",
        )
        query_grads.append(query_part)
        kv_grads.append(lax.psum_scatter(kv_part, "ctx", scatter_dimension=0, tiled=True))
    projected_grad = unturn(
        jnp.concatenate(query_grads, 0), jnp.concatenate(kv_grads, 0), *turns
    )
    normed_grad = times_transposed(projected_grad, qkv_weight[:, : projected_grad.shape[1]])
    _, pull_one = jax.vjp(norm_scale, hidden, gain_pair[0])
    hidden_part, gain_one_grad = pull_one(normed_grad)
    input_grad = attended_grad + hidden_part

    def weight_grads():
        return (
            gain_one_grad,
            gain_two_grad,
            transposed_times(normed, projected_grad),
            transposed_times(mixed_low, out_branch),
            transposed_times(normed_two, gate_up_grad),
            transposed_times(inner_rows, branch_grad),
        )

    return (input_grad, weight_grads)


def on_device(tokens, cotangent, doc_lengths, norm_gains, w_qkv, w_out, w_gate_up, w_down):
    section_index = lax.axis_index("section")
    ctx_index = lax.axis_index("ctx")
    fsdp_count, ctx_count = lax.axis_size("fsdp"), lax.axis_size("ctx")
    micro_count, token_count, width = tokens.shape
    row_count = micro_count * token_count
    qkv_width = w_qkv.shape[2]
    half_ff = w_gate_up.shape[2] // 2
    spare = -(qkv_width + 2) % 128
    first_shard = jnp.concatenate(
        [w_qkv[0], norm_gains[0].T, jnp.zeros((w_qkv.shape[1], spare), jnp.bfloat16)], -1
    )
    shards = (
        first_shard,
        w_out[0],
        w_gate_up[0, :, :half_ff],
        w_gate_up[0, :, half_ff:],
        w_down[0],
    )
    fulls = gather_shards(shards, fsdp_count, ctx_count)
    fulls = [full.reshape(-1, full.shape[-1]) for full in fulls]
    gain_pair = fulls[0][:, qkv_width : qkv_width + 2].T.astype(jnp.float32)
    weights = (
        gain_pair,
        fulls[0],
        fulls[1],
        jnp.concatenate([fulls[2], fulls[3]], -1),
        fulls[4],
    )
    offset = ctx_index * token_count
    seg_k, pos_k = jax.vmap(lambda lengths: layout(lengths, PACK))(doc_lengths[:, 0])
    seg_q = lax.dynamic_slice_in_dim(seg_k, offset, token_count, 1)
    local_pos = lax.dynamic_slice_in_dim(pos_k, offset, token_count, 1).reshape(row_count)
    place = offset + jnp.arange(token_count, dtype=jnp.int32)
    masks = [
        (seg_q[micro][:, None], seg_k[micro][None, :], place[:, None])
        for micro in range(micro_count)
    ]
    half = HD // 2
    frequency = ROPE_BASE ** (-(jnp.arange(half, dtype=jnp.float32) * 2.0 / HD))
    angles = local_pos[:, None] * frequency[None, :]
    cosine, sine = jnp.cos(angles), jnp.sin(angles)
    turns = (
        jnp.concatenate([cosine] * 4, -1),
        jnp.concatenate([-sine, sine, -sine, sine], -1),
    )

    first_input = tokens.reshape(row_count, width)
    first_result, _ = layer_forward(first_input, masks, turns, weights, micro_count)
    incoming = shifted(first_result, "section", 1)
    hidden_in = jnp.where(section_index == 0, first_input, incoming)
    result, saved = layer_forward(hidden_in, masks, turns, weights, micro_count)
    given = cotangent.reshape(row_count, width).astype(jnp.float32)
    last_grad, _ = layer_backward(given, saved, masks, turns, weights, micro_count)
    incoming_grad = shifted(last_grad.astype(jnp.bfloat16), "section", -1)
    upstream = jnp.where(section_index == 1, given, incoming_grad.astype(jnp.float32))
    input_grad, weight_grads = layer_backward(
        upstream, saved, masks, turns, weights, micro_count
    )
    gain_one, gain_two, grad_qkv, grad_out, grad_gate_up, grad_down = weight_grads()
    spare_columns = jnp.zeros((width, spare), jnp.float32)
    first_grad = jnp.concatenate(
        [grad_qkv, gain_one[:, None], gain_two[:, None], spare_columns], -1
    )
    parts = (
        first_grad,
        grad_out,
        grad_gate_up[:, :half_ff],
        grad_gate_up[:, half_ff:],
        grad_down,
    )
    parts = [
        part.astype(jnp.bfloat16).reshape(fsdp_count, ctx_count, -1, part.shape[-1])
        for part in parts
    ]
    totals = reduce_parts(parts, fsdp_count, ctx_count)
    shape = (1, micro_count, token_count, width)
    return (
        result.reshape(shape),
        input_grad.reshape(shape),
        totals[0][None, :, qkv_width],
        totals[0][None, :, qkv_width + 1],
        totals[0][None, :, :qkv_width],
        totals[1][None],
        jnp.concatenate([totals[2], totals[3]], -1)[None],
        totals[4][None],
    )


def solution(mesh):
    return jax.shard_map(
        on_device,
        mesh=mesh,
        in_specs=(
            P(None, ("fsdp", "ctx"), None),
            P(None, ("fsdp", "ctx"), None),
            P(None, "fsdp", None),
            P("section", None, ("fsdp", "ctx")),
            P("section", ("fsdp", "ctx"), None),
            P("section", ("fsdp", "ctx"), None),
            P("section", ("fsdp", "ctx"), None),
            P("section", ("fsdp", "ctx"), None),
        ),
        out_specs=(
            P("section", None, ("fsdp", "ctx"), None),
            P("section", None, ("fsdp", "ctx"), None),
            P("section", ("fsdp", "ctx")),
            P("section", ("fsdp", "ctx")),
            P("section", ("fsdp", "ctx"), None),
            P("section", ("fsdp", "ctx"), None),
            P("section", ("fsdp", "ctx"), None),
            P("section", ("fsdp", "ctx"), None),
        ),
        check_vma=False,
    )
```
